32 devices in a mesh: dp: 4 (over z), expert: 8 (over y, x, core).
Axes of the slice: x: 2, y: 2, z: 4, core: 2. Of those that a mesh axis runs over, the one named last changes fastest.
Arguments:
- tokens: bfloat16 [4096, 768], P(('dp', 'expert')), may hold values from -6 to 6
- qkv_weight: bfloat16 [768, 2304], P(('dp', 'expert')), may hold values from -0.21875 to 0.21875
- out_weight: bfloat16 [768, 768], P(('dp', 'expert')), may hold values from -1.25 to 1.25
- router_weight: bfloat16 [768, 8], P(('dp', 'expert')), may hold values from -0.15625 to 0.15625
- norm_gains: bfloat16 [768, 2], P(('dp', 'expert')), may hold values from 0.5 to 1.5
- bias_table: float32 [32, 12], replicated, may hold values from -6 to 6
- expert_in: bfloat16 [8, 3072, 768], P('expert', 'dp'), may hold values from -0.21875 to 0.21875
- expert_out: bfloat16 [8, 3072, 768], P('expert', 'dp'), may hold values from -3 to 3
- expert_ids: int32 [4096, 1], P(('dp', 'expert')), may hold values from 0 to 7; in each aligned block of 128 rows (0 to 127, 128 to 255, ...) at most 20 rows name the same one
- seq_lengths: int32 [32, 3], P(('dp', 'expert')), may hold values from 1 to 64, 128 in all within a row
- bucket_ids: int32 [127], replicated, may hold values from 0 to 31, as said below
- cotangent: bfloat16 [4096, 768], P(('dp', 'expert')), may hold values from -6 to 6
Outputs:
- mixed_out: bfloat16 [4096, 768], P(('dp', 'expert'))
- grad_tokens: float32 [4096, 768], P(('dp', 'expert'))
- grad_qkv: float32 [768, 2304], P(('dp', 'expert'))
- grad_out: float32 [768, 768], P(('dp', 'expert'))
- grad_router: float32 [768, 8], P(('dp', 'expert'))
- grad_gains: float32 [768, 2], P(('dp', 'expert'))
- grad_table: float32 [32, 12], replicated
- grad_expert_in: float32 [8, 3072, 768], P('expert', 'dp')
- grad_expert_out: float32 [8, 3072, 768], P('expert', 'dp')
The draws below stay inside these ranges and needn't reach their ends.
Inputs may be any that keep to these rules, and one draw needn't show every extreme that they name: `expert_ids`: in each device's 128 rows no expert is named more than 20 times, a bound that some block reaches. `seq_lengths`: each device's 3 lengths sum to 128, the largest is 64. `bucket_ids`: entry r is the bucket of relative position r - 63; every bucket occurs.
All inputs are finite; a program needn't handle non-finite values.
Results may differ from the reference program's by a relative error of at most 0.015.
Values may be sent and summed in bfloat16 or wider, within the bound.
A program may use at most 128 MiB of HBM per device.

```python
import math
import jax
import jax.numpy as jnp
import numpy as np
from jax import lax

D = 768
H = 12
HD = 64
FF = 3072
BUCKETS = 32
TOK_DEV = 128
SEQ_DEV = 3
EXPERTS = 8
TOKENS = 4096
LONGEST = 64
RELS = 127
CAP = 20
DEVICES = 32


def draw_bucket_ids(key, part):
    key = jax.random.fold_in(key, 11)
    first_key, second_key = jax.random.split(key)
    offsets = jnp.arange(RELS, dtype=jnp.int32)
    random_ids = jax.random.randint(first_key, (RELS,), 0, BUCKETS, dtype=jnp.int32)
    merged = jnp.where(offsets < BUCKETS, offsets, random_ids)
    shuffle = jax.random.permutation(second_key, RELS)
    return merged[shuffle].astype(jnp.int32)


def level_of(stream_key, extent, pieces, low, top_value):
    def one(position, shards_of):
        heights = jax.random.uniform(jax.random.fold_in(jax.random.fold_in(stream_key, 6), position), (shards_of,), jnp.float32, low / len(pieces), top_value / len(pieces))
        return jnp.repeat(jnp.exp(heights), extent[position] // shards_of).reshape((-1,) + (1,) * (len(extent) - position - 1))

    level = one(*pieces[0])
    for cut in pieces[1:]:
        level = level * one(*cut)
    return level


def split_up(amount, total, bound, slope):
    weights = [(1 << 20) // math.isqrt(standing ** slope) + 1 for standing in range(2, amount + 1)]
    spare, holding = total - bound - (amount - 1), [1] * (amount - 1)
    while spare > 0:
        free = [i for i in range(amount - 1) if holding[i] < bound]
        pool, left = sum([weights[i] for i in free]), spare
        for i in free:
            addition = min(bound - holding[i], max(1, left * weights[i] // pool), spare)
            holding[i] = holding[i] + addition
            spare = spare - addition
    return np.array([bound] + holding)


def ragged(rng, count, total, reach, slope):
    if count == 2:
        one = jax.random.randint(rng, (), max(1, total - reach), min(reach, total - 1) + 1)
        return jnp.stack([one, total - one])
    sizes = jnp.asarray(split_up(count, total, reach, slope), jnp.int32)
    pairs = (count - 1) // 2
    giver, sink = sizes[1:1 + 2 * pairs:2], sizes[2:2 + 2 * pairs:2]
    margin = jnp.minimum(giver - 1, reach - sink)
    moved = jax.random.randint(jax.random.fold_in(rng, 1), (pairs,), 0, 1 << 20) % (margin + 1)
    sizes = sizes.at[1:1 + 2 * pairs:2].set(giver - moved).at[2:2 + 2 * pairs:2].set(sink + moved)
    return sizes[jax.random.permutation(jax.random.fold_in(rng, 2), count)]


def shared_out(key, own, number, rows, amount, top, reach, skew):
    order = jax.random.permutation(key, amount)
    packed, usual = portions_of(amount, rows * top, reach, skew, True), portions_of(amount, rows * top, reach, skew, False)
    places = jnp.arange(amount)

    def named(lengths, offset_by):
        used = int((lengths > 0).sum())
        fixed = max(1, used // 4)
        shifted = fixed + (places - fixed + offset_by * (used - fixed)) % max(1, amount - fixed)
        return jnp.zeros((amount,), jnp.int32).at[order[jnp.where(places < fixed, places, shifted)]].set(jnp.asarray(lengths, jnp.int32))

    lengths = jnp.where(number % 4 == 0, named(packed, number // 4), named(usual, number - number // 4 - 1))
    mixed = jax.random.permutation(jax.random.fold_in(own, 3), amount)
    donor, taker = mixed[0:amount // 2 * 2:2], mixed[1:amount // 2 * 2:2]
    room = jnp.minimum(lengths[donor] - 1, reach - lengths[taker]) // 2
    room = jnp.where((donor == order[0]) | (taker == order[0]) | (lengths[taker] == 0), 0, jnp.maximum(room, 0))
    shifted = jax.random.randint(jax.random.fold_in(own, 4), (amount // 2,), 0, 1 << 20) % (room + 1)
    lengths = lengths.at[donor].add(-shifted).at[taker].add(shifted)
    items = jnp.searchsorted(jnp.cumsum(lengths), jnp.arange(rows * top), side="right").astype(jnp.int32)
    grid = items.reshape(top, rows).T
    grid = grid[jax.random.permutation(jax.random.fold_in(own, 1), rows)]
    offset_by = jax.random.randint(jax.random.fold_in(own, 2), (rows, 1), 0, top)
    return jnp.take_along_axis(grid, (jnp.arange(top)[None, :] + offset_by) % top, axis=1)


def portions_of(count, total, most, lean, full):
    loads = [(1 << 20) // math.isqrt(grade ** lean) + 1 for grade in range(1, count + 1)]
    largest = most if full else min(most, max(-(-total // count), total * loads[0] // sum(loads)))
    least = 1 if total - largest >= count - 1 else 0
    counts, spare = [largest] + [least] * (count - 1), total - largest - least * (count - 1)
    while spare > 0:
        movable = [i for i in range(1, count) if counts[i] < largest] or [i for i in range(1, count) if counts[i] < most]
        whole, left = sum([loads[i] for i in movable]), spare
        for i in movable:
            more = min(most - counts[i], max(1, left * loads[i] // whole), spare)
            counts[i] = counts[i] + more
            spare = spare - more
    return np.array(counts)


def bell_draw(own_key, shape, deviation, most, shards=(), kind=jnp.bfloat16):
    values = deviation * jax.random.normal(own_key, shape, jnp.float32)
    if shards:
        values = values * level_of(own_key, shape, shards, -0.22, 0.18)
    return jnp.clip(values, -most, most).astype(kind)


def setup_inputs(seed: int = 0) -> dict:
    key_list = jax.random.split(jax.random.key(seed), 13)
    tokens = bell_draw(key_list[0], (TOKENS, D), 1.0, 6.0, ((0, 32),))
    qkv_weight = bell_draw(key_list[1], (D, 3 * D), D ** -0.5, 0.21875, ((0, 32),))
    out_weight = bell_draw(key_list[2], (D, D), (D // 32) ** -0.5, 1.25, ((0, 32),))
    router_weight = bell_draw(key_list[3], (D, EXPERTS), (2 * D) ** -0.5, 0.15625, ((0, 32),))
    norm_gains = jnp.clip(1.0 + 0.1 * jax.random.normal(key_list[4], (D, 2), jnp.float32), 0.5, 1.5).astype(jnp.bfloat16)
    bias_table = bell_draw(key_list[5], (BUCKETS, H), 1.0, 6.0, (), jnp.float32)
    expert_in = bell_draw(key_list[6], (EXPERTS, FF, D), D ** -0.5, 0.21875, ((0, 8), (1, 4)))
    expert_out = bell_draw(key_list[7], (EXPERTS, FF, D), (EXPERTS * 1.5 * FF ** -0.5), 3.0, ((0, 8), (1, 4)))
    expert_ids_keys = jax.random.split(jax.random.fold_in(key_list[8], 1), TOKENS // TOK_DEV)
    expert_ids_turns = jax.random.permutation(jax.random.fold_in(key_list[8], 3), TOKENS // TOK_DEV)
    expert_ids = jax.vmap(lambda own, number: shared_out(jax.random.fold_in(key_list[8], 2), own, number, TOK_DEV, EXPERTS, 1, CAP, 2))(expert_ids_keys, expert_ids_turns).reshape((TOKENS, 1))
    seq_lengths = jax.vmap(lambda own: ragged(own, SEQ_DEV, TOK_DEV, LONGEST, 0))(jax.random.split(key_list[9], DEVICES)).reshape((DEVICES, SEQ_DEV)).astype(jnp.int32)
    bucket_ids = draw_bucket_ids(jax.random.fold_in(key_list[12], 71), 0)
    cotangent = bell_draw(key_list[11], (TOKENS, D), 1.0, 6.0, ((0, 32),))
    return {"tokens": tokens, "qkv_weight": qkv_weight, "out_weight": out_weight, "router_weight": router_weight, "norm_gains": norm_gains, "bias_table": bias_table, "expert_in": expert_in, "expert_out": expert_out, "expert_ids": expert_ids, "seq_lengths": seq_lengths, "bucket_ids": bucket_ids, "cotangent": cotangent}


EPSILON = 1e-06
NEGATIVE = -1e+30
PRECISE = lax.Precision.HIGHEST

@jax.custom_vjp
def low(v):
    return lax.optimization_barrier(v.astype(jnp.bfloat16)).astype(jnp.float32)

@jax.custom_vjp
def low_back(v):
    return v

def low_keep(v):
    return (low(v), None)

def low_pass(kept, grad):
    return (grad,)

def back_keep(v):
    return (v, None)

def back_low(kept, grad):
    return (low(grad),)
low.defvjp(low_keep, low_pass)
low_back.defvjp(back_keep, back_low)

def rms_scale(values, norm_gain):
    inverse = lax.rsqrt(lax.optimization_barrier(jnp.mean(values * values, axis=-1, keepdims=True)) + EPSILON)
    return values * inverse * norm_gain

def segment_of(lengths_row):
    seq_ends = jnp.cumsum(lengths_row).astype(jnp.int32)
    positions = jnp.arange(TOK_DEV, dtype=jnp.int32)
    return lax.optimization_barrier(jnp.sum((positions[:, None] >= seq_ends[None, :]).astype(jnp.int32), axis=1))

def relative_index():
    positions = jnp.arange(TOK_DEV, dtype=jnp.int32)
    offsets = jnp.clip(positions[None, :] - positions[:, None], -(LONGEST - 1), LONGEST - 1)
    return (offsets + (LONGEST - 1)).astype(jnp.int32)

def attention_block(token_block, segment, qkv_w, out_w, norm_gain, rel_bias):
    normed = low(rms_scale(token_block, norm_gain))
    qkv_rows = low(low_back(jnp.dot(normed, qkv_w, precision=PRECISE)))
    queries = qkv_rows[:, :D].reshape(TOK_DEV, H, HD)
    all_keys = qkv_rows[:, D:2 * D].reshape(TOK_DEV, H, HD)
    value_rows = qkv_rows[:, 2 * D:].reshape(TOK_DEV, H, HD)
    raw_score = low_back(jnp.einsum('qhe,khe->hqk', queries, all_keys, precision=PRECISE) * HD ** (-0.5))
    pos_bias = rel_bias[:, relative_index()]
    same_doc = segment[:, None] == segment[None, :]
    scores = jnp.where(same_doc[None], raw_score + pos_bias, NEGATIVE)
    row_top = lax.optimization_barrier(jnp.max(scores, axis=-1, keepdims=True))
    exp_scores = jnp.exp(scores - row_top)
    attn_probs = low(exp_scores / lax.optimization_barrier(jnp.sum(exp_scores, axis=-1, keepdims=True)))
    attended = jnp.einsum('hqk,khe->qhe', attn_probs, value_rows, precision=PRECISE).reshape(TOK_DEV, D)
    attended = low(low_back(attended))
    return token_block + low_back(jnp.dot(attended, out_w, precision=PRECISE))

def expert_block(triple):
    expert_token_rows, weight_in, weight_out = triple
    before_activation = low_back(jnp.einsum('rd,fd->rf', expert_token_rows, weight_in, precision=PRECISE))
    hidden_activations = low(jax.nn.gelu(before_activation))
    return low(low_back(jnp.dot(hidden_activations, weight_out, precision=PRECISE)))

def reference(tokens, qkv_weight, out_weight, router_weight, norm_gains, bias_table, expert_in, expert_out, expert_ids, seq_lengths, bucket_ids, cotangent):
    segments = jax.vmap(segment_of)(seq_lengths)
    chosen = expert_ids[:, 0].reshape(DEVICES, TOK_DEV).astype(jnp.int32)
    picked = (chosen[..., None] == jnp.arange(EXPERTS, dtype=jnp.int32)).astype(jnp.int32)
    earlier = jnp.cumsum(picked, axis=1) - picked
    slot_in = lax.optimization_barrier(jnp.sum(earlier * picked, axis=-1))
    flat_slot = (chosen * CAP + slot_in).astype(jnp.int32)
    device_row = jnp.broadcast_to(jnp.arange(DEVICES, dtype=jnp.int32)[:, None], (DEVICES, TOK_DEV))
    picked_f = picked.astype(jnp.float32)

    def forward(token_f, qkv_w, out_w, router_w, gains_f, table_f, weight_in, weight_out):
        rel_bias = jnp.transpose(table_f[bucket_ids])
        blocks = token_f.reshape(DEVICES, TOK_DEV, D)

        def one_block(paired):
            return attention_block(paired[0], paired[1], qkv_w, out_w, gains_f[:, 0], rel_bias)
        residual = lax.map(jax.checkpoint(one_block), (blocks, segments))
        normed = low(rms_scale(residual, gains_f[:, 1]))
        logits = low_back(jnp.einsum('btd,de->bte', normed, router_w, precision=PRECISE))
        logit_top = lax.optimization_barrier(jnp.max(logits, axis=-1, keepdims=True))
        exp_logits = jnp.exp(logits - logit_top)
        route_probs = exp_logits / lax.optimization_barrier(jnp.sum(exp_logits, axis=-1, keepdims=True))
        gate_value = lax.optimization_barrier(jnp.sum(route_probs * picked_f, axis=-1, keepdims=True))
        buffer_rows = jnp.zeros((DEVICES, EXPERTS * CAP, D), jnp.float32)
        buffer_rows = low_back(buffer_rows.at[device_row, flat_slot].set(normed))
        per_expert = buffer_rows.reshape(DEVICES, EXPERTS, CAP, D).transpose(1, 0, 2, 3).reshape(EXPERTS, DEVICES * CAP, D)
        returned = lax.map(jax.checkpoint(expert_block), (per_expert, weight_in, weight_out))
        back_rows = returned.reshape(EXPERTS, DEVICES, CAP, D).transpose(1, 0, 2, 3).reshape(DEVICES, EXPERTS * CAP, D)
        gathered = back_rows[device_row, flat_slot]
        return (residual + gate_value * gathered).reshape(TOKENS, D)
    primal = (tokens.astype(jnp.float32), qkv_weight.astype(jnp.float32), out_weight.astype(jnp.float32), router_weight.astype(jnp.float32), norm_gains.astype(jnp.float32), bias_table.astype(jnp.float32), expert_in.astype(jnp.float32), expert_out.astype(jnp.float32))
    result, pullback = jax.vjp(forward, *primal)
    grads = pullback(cotangent.astype(jnp.float32))
    return (result.astype(jnp.bfloat16), grads[0], grads[1], grads[2], grads[3], grads[4], grads[5], grads[6], grads[7])
```

```python
import functools

import jax
import jax.numpy as jnp
from jax import lax
from jax.experimental import pallas as pl
from jax.experimental.pallas import tpu as pltpu
from jax.sharding import PartitionSpec as P

H = 12
HD = 64
BUCKETS = 32
LANES = 128
EPSILON = 1e-06
NEGATIVE = -1e30
PRECISE = lax.Precision.HIGHEST
F32 = jnp.float32
BF16 = jnp.bfloat16
VMEM = pltpu.VMEM
BIG = 56 * 1024 * 1024


def mm(a, b, dims=((1,), (0,)), precision=None):
    return lax.dot_general(a, b, (dims, ((), ())), preferred_element_type=F32, precision=precision)


NT = ((1,), (1,))
TN = ((0,), (0,))


def rms_inverse(values):
    return lax.rsqrt(jnp.mean(values * values, axis=-1, keepdims=True) + EPSILON)


def placement(ids, experts, capacity):
    rows = ids.shape[0]
    picked = (ids == lax.broadcasted_iota(jnp.int32, (rows, experts), 1)).astype(F32)
    before = lax.broadcasted_iota(jnp.int32, (rows, rows), 1) < lax.broadcasted_iota(
        jnp.int32, (rows, rows), 0
    )
    earlier = mm(before.astype(BF16), picked.astype(BF16))
    slot = jnp.sum(earlier * picked, axis=-1, keepdims=True).astype(jnp.int32)
    flat = ids * capacity + slot
    place = (flat == lax.broadcasted_iota(jnp.int32, (rows, experts * capacity), 1)).astype(BF16)
    return picked, place


def forward_kernel(
    model_dim, experts, capacity,
    lens_ref, tok_ref, w_ref, gains_ref, rel_ref, ids_ref, cot_ref,
    normed_ref, qkv_ref, probs_ref, att_ref, res_ref, route_ref, send_ref,
):
    d = model_dim
    rows = tok_ref.shape[0]
    x = tok_ref[...].astype(F32)
    normed_ref[...] = (x * rms_inverse(x) * gains_ref[0:1, :]).astype(BF16)
    for c in range(0, 3 * d, 256):
        qkv_ref[:, c : c + 256] = mm(normed_ref[...], w_ref[:, c : c + 256]).astype(BF16)
    first = lens_ref[0, 0]
    second = first + lens_ref[0, 1]

    def segment(axis):
        pos = lax.broadcasted_iota(jnp.int32, (rows, rows), axis)
        return (pos >= first).astype(jnp.int32) + (pos >= second).astype(jnp.int32)

    same = segment(0) == segment(1)
    lane = lax.broadcasted_iota(jnp.int32, (rows, LANES), 1)
    for pair in range(H // 2):
        at = pair * LANES
        q = qkv_ref[:, at : at + LANES]
        k = qkv_ref[:, d + at : d + at + LANES]
        v = qkv_ref[:, 2 * d + at : 2 * d + at + LANES]
        outs = []
        for half in range(2):
            h = 2 * pair + half
            mine = (lane >= HD) if half else (lane < HD)
            bias = pltpu.roll(
                jnp.broadcast_to(rel_ref[h : h + 1, :], (rows, LANES)), 0, 1, stride=1, stride_axis=0
            )
            scores = mm(jnp.where(mine, q, jnp.zeros_like(q)), k, NT) * (HD ** (-0.5)) + bias
            scores = jnp.where(same, scores, NEGATIVE)
            e = jnp.exp(scores - jnp.max(scores, axis=-1, keepdims=True))
            p = e / jnp.sum(e, axis=-1, keepdims=True)
            probs_ref[h] = p
            outs.append(mm(p.astype(BF16), v))
        att_ref[:, at : at + LANES] = jnp.where(lane < HD, outs[0], outs[1]).astype(BF16)
    res = x + mm(att_ref[...], w_ref[:, 3 * d : 4 * d])
    res_ref[...] = res
    routed = (res * rms_inverse(res) * gains_ref[1:2, :]).astype(BF16)
    logits = mm(routed, w_ref[:, 4 * d :])[:, :experts]
    e = jnp.exp(logits - jnp.max(logits, axis=-1, keepdims=True))
    route = e / jnp.sum(e, axis=-1, keepdims=True)
    route_ref[...] = route
    picked, place = placement(ids_ref[...], experts, capacity)
    gate = jnp.sum(route * picked, axis=-1, keepdims=True)
    grad_comb = (gate * cot_ref[...].astype(F32)).astype(BF16)
    send_ref[:, :d] = mm(place, routed, TN).astype(BF16)
    send_ref[:, d:] = mm(place, grad_comb, TN).astype(BF16)


def backward_kernel(
    model_dim, experts, capacity,
    tok_ref, w_ref, gains_ref, ids_ref, cot_ref,
    normed_ref, qkv_ref, probs_ref, att_ref, res_ref, route_ref, ret_ref,
    mixed_ref, gtok_ref, grads_ref, grel_ref, grows_ref,
):
    d = model_dim
    rows = tok_ref.shape[0]
    x = tok_ref[...].astype(F32)
    g = cot_ref[...].astype(F32)
    res = res_ref[...]
    route = route_ref[...]
    picked, place = placement(ids_ref[...], experts, capacity)
    gate = jnp.sum(route * picked, axis=-1, keepdims=True)
    combined = mm(place, ret_ref[:, :d])
    mixed_ref[...] = (res + gate * combined).astype(BF16)
    grad_gate = jnp.sum(g * combined, axis=-1, keepdims=True)
    misc = w_ref.shape[1] - 4 * d
    glog = (grad_gate * gate * (picked - route)).astype(BF16)
    glog = jnp.concatenate([glog, jnp.zeros((rows, misc - experts), BF16)], axis=1)
    grouted = mm(place, ret_ref[:, d:]) + mm(glog, w_ref[:, 4 * d :], NT)
    inv2 = rms_inverse(res)
    scaled2 = res * inv2
    gain2 = gains_ref[1:2, :]
    routed = (scaled2 * gain2).astype(BF16)
    w = grouted * gain2
    gres = g + inv2 * (w - scaled2 * jnp.mean(w * scaled2, axis=-1, keepdims=True))
    col = lax.broadcasted_iota(jnp.int32, (rows, misc), 1)
    small = mm(routed, glog, TN) + mm(
        grouted * scaled2, (col == experts + 1).astype(F32), TN, PRECISE
    )
    branch = gres.astype(BF16)
    grads_ref[:, 3 * d : 4 * d] = mm(att_ref[...], branch, TN).astype(BF16)
    gatt = mm(branch, w_ref[:, 3 * d : 4 * d], NT).astype(BF16)
    lane = lax.broadcasted_iota(jnp.int32, (rows, LANES), 1)
    line = lax.broadcasted_iota(jnp.int32, (rows, LANES), 0)
    scale = HD ** (-0.5)
    for pair in range(H // 2):
        at = pair * LANES
        q = qkv_ref[:, at : at + LANES]
        k = qkv_ref[:, d + at : d + at + LANES]
        v = qkv_ref[:, 2 * d + at : 2 * d + at + LANES]
        ga = gatt[:, at : at + LANES]
        gq, gk, gv = [], [], []
        for half in range(2):
            h = 2 * pair + half
            mine = (lane >= HD) if half else (lane < HD)
            p = probs_ref[h]
            gp = mm(jnp.where(mine, ga, jnp.zeros_like(ga)), v, NT)
            gs = p * (gp - jnp.sum(p * gp, axis=-1, keepdims=True))
            low = gs.astype(BF16)
            gv.append(mm(p.astype(BF16), ga, TN))
            gq.append(mm(low, k) * scale)
            gk.append(mm(low, q, TN) * scale)
            step = 1
            while step < rows:
                turned = pltpu.roll(gs, LANES - step, 1)
                gs = jnp.where((line & step) != 0, turned, gs)
                step *= 2
            grel_ref[h : h + 1, :] = jnp.sum(gs, axis=0, keepdims=True)
        for base, two in ((0, gq), (d, gk), (2 * d, gv)):
            grows_ref[:, base + at : base + at + LANES] = jnp.where(
                lane < HD, two[0], two[1]
            ).astype(BF16)
    for c in range(0, 3 * d, 256):
        grads_ref[:, c : c + 256] = mm(normed_ref[...], grows_ref[:, c : c + 256], TN).astype(BF16)
    gnorm = mm(grows_ref[...], w_ref[:, : 3 * d], NT)
    inv1 = rms_inverse(x)
    scaled1 = x * inv1
    w = gnorm * gains_ref[0:1, :]
    gtok_ref[...] = gres + inv1 * (w - scaled1 * jnp.mean(w * scaled1, axis=-1, keepdims=True))
    small = small + mm(gnorm * scaled1, (col == experts).astype(F32), TN, PRECISE)
    grads_ref[:, 4 * d :] = small.astype(BF16)


def gather_weights(packed):
    return lax.all_gather(packed, ("dp", "expert"), axis=0, tiled=True)


def scatter_grads(grads):
    return lax.psum_scatter(grads, ("dp", "expert"), scatter_dimension=0, tiled=True).astype(F32)


def dispatch(send, experts, capacity):
    peers = lax.axis_size("expert")
    width = send.shape[1]
    arrived = lax.all_to_all(
        send.reshape(experts, capacity, width), "expert", split_axis=0, concat_axis=0, tiled=True
    )
    local_count = experts // peers
    grouped = jnp.transpose(
        arrived.reshape(peers, local_count, capacity, width), (1, 0, 2, 3)
    ).reshape(local_count, peers * capacity, width)
    return lax.all_gather(grouped, "dp", axis=1, tiled=True)


def collect(partial, experts, capacity):
    peers = lax.axis_size("expert")
    width = partial.shape[-1]
    local_count = experts // peers
    mine = lax.psum_scatter(partial, "dp", scatter_dimension=1, tiled=True)
    grouped = jnp.transpose(
        mine.reshape(local_count, peers, capacity, width), (1, 0, 2, 3)
    ).reshape(experts, capacity, width)
    back = lax.all_to_all(grouped, "expert", split_axis=0, concat_axis=0, tiled=True)
    return back.reshape(experts * capacity, width)


def local(
    tokens, qkv_weight, out_weight, router_weight, norm_gains, bias_table,
    expert_in, expert_out, expert_ids, seq_lengths, bucket_ids, cotangent,
):
    rows, d = tokens.shape
    experts = router_weight.shape[1]
    shard = qkv_weight.shape[0]
    parts = d // shard
    capacity = max(2, 5 * rows // (4 * experts))
    table_cols = -(-BUCKETS * H // shard)
    used = experts + 2 + table_cols
    misc = -(-used // LANES) * LANES
    total = 4 * d + misc

    packed = jnp.concatenate(
        [qkv_weight, out_weight, router_weight, norm_gains,
         jnp.zeros((shard, misc - experts - 2), BF16)], axis=1,
    )
    weights = gather_weights(packed)
    gains = jnp.transpose(weights[:, 4 * d + experts : 4 * d + experts + 2]).astype(F32)
    half = rows // 2
    ring = jnp.concatenate(
        [bucket_ids[half - 1 :], jnp.full((1,), -1, jnp.int32), bucket_ids[: half - 1]]
    )
    hot = (ring[None, :] == jnp.arange(BUCKETS, dtype=jnp.int32)[:, None]).astype(F32)
    rel = lax.dot_general(bias_table, hot, (((0,), (0,)), ((), ())), precision=PRECISE)

    kept_shapes = (
        jax.ShapeDtypeStruct((rows, d), BF16),
        jax.ShapeDtypeStruct((rows, 3 * d), BF16),
        jax.ShapeDtypeStruct((H, rows, rows), F32),
        jax.ShapeDtypeStruct((rows, d), BF16),
        jax.ShapeDtypeStruct((rows, d), F32),
        jax.ShapeDtypeStruct((rows, experts), F32),
        jax.ShapeDtypeStruct((experts * capacity, 2 * d), BF16),
    )
    vm = pl.BlockSpec(memory_space=VMEM)
    *kept, send = pl.pallas_call(
        functools.partial(forward_kernel, d, experts, capacity),
        out_shape=kept_shapes,
        in_specs=[pl.BlockSpec(memory_space=pltpu.SMEM)] + [vm] * 6,
        out_specs=[vm] * 7,
        compiler_params=pltpu.CompilerParams(vmem_limit_bytes=BIG),
        name="attention_forward",
    )(seq_lengths, tokens, weights, gains, rel, expert_ids, cotangent)

    both = dispatch(send, experts, capacity)
    rows_in, grad_in = both[..., :d], both[..., d:]
    pre = jnp.einsum("aou,ahu->aoh", rows_in, expert_in, preferred_element_type=F32)
    act, act_back = jax.vjp(jax.nn.gelu, pre)
    hidden = act.astype(BF16)
    grad_hidden = jnp.einsum("aou,ahu->aoh", grad_in, expert_out, preferred_element_type=F32)
    grad_pre = act_back(grad_hidden)[0].astype(BF16)
    part_out = jnp.einsum("ziq,zqb->zib", hidden, expert_out, preferred_element_type=F32)
    part_grad = jnp.einsum("ziq,zqb->zib", grad_pre, expert_in, preferred_element_type=F32)
    partial = jnp.concatenate([part_out.astype(BF16), part_grad.astype(BF16)], axis=-1)
    ret = collect(partial, experts, capacity)
    grad_expert_in = jnp.einsum("ieq,ieo->iqo", grad_pre, rows_in, preferred_element_type=F32)
    grad_expert_out = jnp.einsum("ieq,ieo->iqo", hidden, grad_in, preferred_element_type=F32)

    mixed, grad_tokens, grads, grel = pl.pallas_call(
        functools.partial(backward_kernel, d, experts, capacity),
        out_shape=(
            jax.ShapeDtypeStruct((rows, d), BF16),
            jax.ShapeDtypeStruct((rows, d), F32),
            jax.ShapeDtypeStruct((d, total), BF16),
            jax.ShapeDtypeStruct((H, LANES), F32),
        ),
        in_specs=[vm] * 12,
        out_specs=[vm] * 4,
        scratch_shapes=[VMEM((rows, 3 * d), BF16)],
        compiler_params=pltpu.CompilerParams(vmem_limit_bytes=BIG),
        name="attention_backward",
    )(tokens, weights, gains, expert_ids, cotangent, *kept, ret)

    table = lax.dot_general(hot, grel, (((1,), (1,)), ((), ())), precision=PRECISE)
    tile = jnp.pad(table.reshape(-1), (0, shard * table_cols - BUCKETS * H))
    tile = jnp.tile(tile.reshape(shard, table_cols).astype(BF16), (parts, 1))
    grads = lax.dynamic_update_slice(grads, tile, (0, 4 * d + experts + 2))
    summed = scatter_grads(grads)
    at = 4 * d + experts
    table_sum = summed[:, at + 2 : at + 2 + table_cols].reshape(-1)[: BUCKETS * H]
    return (
        mixed,
        grad_tokens,
        summed[:, : 3 * d],
        summed[:, 3 * d : 4 * d],
        summed[:, 4 * d : at],
        summed[:, at : at + 2],
        table_sum.reshape(BUCKETS, H),
        grad_expert_in,
        grad_expert_out,
    )


def solution(mesh):
    both = P(("dp", "expert"), None)
    wide = P("expert", "dp", None)
    return jax.shard_map(
        local,
        mesh=mesh,
        in_specs=(both, both, both, both, both, P(), wide, wide, both, both, P(), both),
        out_specs=(both, both, both, both, both, both, P(), wide, wide),
        check_vma=False,
    )
```

```python
import functools

import jax
import jax.numpy as jnp
from jax import lax
from jax.experimental import pallas as pl
from jax.experimental.pallas import tpu as pltpu
from jax.sharding import PartitionSpec as P

H = 12
HD = 64
BUCKETS = 32
LANES = 128
EPSILON = 1e-06
NEGATIVE = -1e30
PRECISE = lax.Precision.HIGHEST
F32 = jnp.float32
BF16 = jnp.bfloat16
VMEM = pltpu.VMEM
BIG = 56 * 1024 * 1024


def mm(a, b, dims=((1,), (0,)), precision=None):
    return lax.dot_general(a, b, (dims, ((), ())), preferred_element_type=F32, precision=precision)


NT = ((1,), (1,))
TN = ((0,), (0,))


def rms_inverse(values):
    return lax.rsqrt(jnp.mean(values * values, axis=-1, keepdims=True) + EPSILON)


def placement(ids, experts, capacity):
    rows = ids.shape[0]
    picked = (ids == lax.broadcasted_iota(jnp.int32, (rows, experts), 1)).astype(F32)
    before = lax.broadcasted_iota(jnp.int32, (rows, rows), 1) < lax.broadcasted_iota(
        jnp.int32, (rows, rows), 0
    )
    earlier = mm(before.astype(BF16), picked.astype(BF16))
    slot = jnp.sum(earlier * picked, axis=-1, keepdims=True).astype(jnp.int32)
    flat = ids * capacity + slot
    place = (flat == lax.broadcasted_iota(jnp.int32, (rows, experts * capacity), 1)).astype(BF16)
    return picked, place


def forward_kernel(
    model_dim, experts, capacity,
    lens_ref, tok_ref, w_ref, gains_ref, rel_ref, ids_ref, cot_ref,
    normed_ref, qkv_ref, probs_ref, att_ref, res_ref, route_ref, send_ref,
):
    d = model_dim
    rows = tok_ref.shape[0]
    x = tok_ref[...].astype(F32)
    normed_ref[...] = (x * rms_inverse(x) * gains_ref[0:1, :]).astype(BF16)
    for c in range(0, 3 * d, 256):
        qkv_ref[:, c : c + 256] = mm(normed_ref[...], w_ref[:, c : c + 256]).astype(BF16)
    first = lens_ref[0, 0]
    second = first + lens_ref[0, 1]

    def segment(axis):
        pos = lax.broadcasted_iota(jnp.int32, (rows, rows), axis)
        return (pos >= first).astype(jnp.int32) + (pos >= second).astype(jnp.int32)

    same = segment(0) == segment(1)
    lane = lax.broadcasted_iota(jnp.int32, (rows, LANES), 1)
    for pair in range(H // 2):
        at = pair * LANES
        q = qkv_ref[:, at : at + LANES]
        k = qkv_ref[:, d + at : d + at + LANES]
        v = qkv_ref[:, 2 * d + at : 2 * d + at + LANES]
        outs = []
        for half in range(2):
            h = 2 * pair + half
            mine = (lane >= HD) if half else (lane < HD)
            bias = pltpu.roll(
                jnp.broadcast_to(rel_ref[h : h + 1, :], (rows, LANES)), 0, 1, stride=1, stride_axis=0
            )
            scores = mm(jnp.where(mine, q, jnp.zeros_like(q)), k, NT) * (HD ** (-0.5)) + bias
            scores = jnp.where(same, scores, NEGATIVE)
            e = jnp.exp(scores - jnp.max(scores, axis=-1, keepdims=True))
            p = e / jnp.sum(e, axis=-1, keepdims=True)
            probs_ref[h] = p
            outs.append(mm(p.astype(BF16), v))
        att_ref[:, at : at + LANES] = jnp.where(lane < HD, outs[0], outs[1]).astype(BF16)
    res = x + mm(att_ref[...], w_ref[:, 3 * d : 4 * d])
    res_ref[...] = res
    routed = (res * rms_inverse(res) * gains_ref[1:2, :]).astype(BF16)
    logits = mm(routed, w_ref[:, 4 * d :])[:, :experts]
    e = jnp.exp(logits - jnp.max(logits, axis=-1, keepdims=True))
    route = e / jnp.sum(e, axis=-1, keepdims=True)
    route_ref[...] = route
    picked, place = placement(ids_ref[...], experts, capacity)
    gate = jnp.sum(route * picked, axis=-1, keepdims=True)
    grad_comb = (gate * cot_ref[...].astype(F32)).astype(BF16)
    send_ref[:, :d] = mm(place, routed, TN).astype(BF16)
    send_ref[:, d:] = mm(place, grad_comb, TN).astype(BF16)


def backward_kernel(
    model_dim, experts, capacity,
    tok_ref, w_ref, gains_ref, ids_ref, cot_ref,
    normed_ref, qkv_ref, probs_ref, att_ref, res_ref, route_ref, ret_ref,
    mixed_ref, gtok_ref, grads_ref, grel_ref, grows_ref,
):
    d = model_dim
    rows = tok_ref.shape[0]
    x = tok_ref[...].astype(F32)
    g = cot_ref[...].astype(F32)
    res = res_ref[...]
    route = route_ref[...]
    picked, place = placement(ids_ref[...], experts, capacity)
    gate = jnp.sum(route * picked, axis=-1, keepdims=True)
    combined = mm(place, ret_ref[:, :d])
    mixed_ref[...] = (res + gate * combined).astype(BF16)
    grad_gate = jnp.sum(g * combined, axis=-1, keepdims=True)
    misc = w_ref.shape[1] - 4 * d
    glog = (grad_gate * gate * (picked - route)).astype(BF16)
    glog = jnp.concatenate([glog, jnp.zeros((rows, misc - experts), BF16)], axis=1)
    grouted = mm(place, ret_ref[:, d:]) + mm(glog, w_ref[:, 4 * d :], NT)
    inv2 = rms_inverse(res)
    scaled2 = res * inv2
    gain2 = gains_ref[1:2, :]
    routed = (scaled2 * gain2).astype(BF16)
    w = grouted * gain2
    gres = g + inv2 * (w - scaled2 * jnp.mean(w * scaled2, axis=-1, keepdims=True))
    col = lax.broadcasted_iota(jnp.int32, (rows, misc), 1)
    small = mm(routed, glog, TN) + mm(
        grouted * scaled2, (col == experts + 1).astype(F32), TN, PRECISE
    )
    branch = gres.astype(BF16)
    grads_ref[:, 3 * d : 4 * d] = mm(att_ref[...], branch, TN).astype(BF16)
    gatt = mm(branch, w_ref[:, 3 * d : 4 * d], NT).astype(BF16)
    lane = lax.broadcasted_iota(jnp.int32, (rows, LANES), 1)
    line = lax.broadcasted_iota(jnp.int32, (rows, LANES), 0)
    scale = HD ** (-0.5)
    for pair in range(H // 2):
        at = pair * LANES
        q = qkv_ref[:, at : at + LANES]
        k = qkv_ref[:, d + at : d + at + LANES]
        v = qkv_ref[:, 2 * d + at : 2 * d + at + LANES]
        ga = gatt[:, at : at + LANES]
        gq, gk, gv = [], [], []
        for half in range(2):
            h = 2 * pair + half
            mine = (lane >= HD) if half else (lane < HD)
            p = probs_ref[h]
            gp = mm(jnp.where(mine, ga, jnp.zeros_like(ga)), v, NT)
            gs = p * (gp - jnp.sum(p * gp, axis=-1, keepdims=True))
            low = gs.astype(BF16)
            gv.append(mm(p.astype(BF16), ga, TN))
            gq.append(mm(low, k) * scale)
            gk.append(mm(low, q, TN) * scale)
            step = 1
            while step < rows:
                turned = pltpu.roll(gs, LANES - step, 1)
                gs = jnp.where((line & step) != 0, turned, gs)
                step *= 2
            grel_ref[h : h + 1, :] = jnp.sum(gs, axis=0, keepdims=True)
        for base, two in ((0, gq), (d, gk), (2 * d, gv)):
            grows_ref[:, base + at : base + at + LANES] = jnp.where(
                lane < HD, two[0], two[1]
            ).astype(BF16)
    for c in range(0, 3 * d, 256):
        grads_ref[:, c : c + 256] = mm(normed_ref[...], grows_ref[:, c : c + 256], TN).astype(BF16)
    gnorm = mm(grows_ref[...], w_ref[:, : 3 * d], NT)
    inv1 = rms_inverse(x)
    scaled1 = x * inv1
    w = gnorm * gains_ref[0:1, :]
    gtok_ref[...] = gres + inv1 * (w - scaled1 * jnp.mean(w * scaled1, axis=-1, keepdims=True))
    small = small + mm(gnorm * scaled1, (col == experts).astype(F32), TN, PRECISE)
    grads_ref[:, 4 * d :] = small.astype(BF16)


CORES = 2
MESH = pl.DeviceIdType.MESH


def places():
    experts_axis = lax.axis_size("expert")
    sizes = {"dp": lax.axis_size("dp"), "chip": experts_axis // CORES, "core": CORES,
             "expert": experts_axis}
    e = lax.axis_index("expert")
    here = {"dp": lax.axis_index("dp"), "chip": e // CORES, "core": lax.rem(e, CORES), "expert": e}
    return sizes, here


def peer_of(here, axis, other):
    if axis == "dp":
        return (other, here["expert"])
    if axis == "chip":
        return (here["dp"], other * CORES + here["core"])
    if axis == "core":
        return (here["dp"], here["chip"] * CORES + other)
    return (here["dp"], other)


def greet(sizes, here, axes):
    barrier = pltpu.get_barrier_semaphore()
    count = 0
    for axis in axes:
        for k in range(1, sizes[axis]):
            other = lax.rem(here[axis] + k, sizes[axis])
            pl.semaphore_signal(
                barrier, inc=1, device_id=peer_of(here, axis, other), device_id_type=MESH
            )
            count += 1
    pl.semaphore_wait(barrier, count)


def send_all(sizes, here, axis, source, target, send_sem, recv_sem, base):
    copies = []
    for k in range(1, sizes[axis]):
        other = lax.rem(here[axis] + k, sizes[axis])
        copy = pltpu.make_async_remote_copy(
            src_ref=source(other), dst_ref=target,
            send_sem=send_sem.at[base + k - 1], recv_sem=recv_sem.at[base + k - 1],
            device_id=peer_of(here, axis, other), device_id_type=MESH,
        )
        copy.start()
        copies.append(copy)
    return copies


def weights_kernel(x_ref, out_ref, send_sem, recv_sem, own_sem):
    sizes, here = places()
    dp, chip, core = here["dp"], here["chip"], here["core"]
    own = pltpu.make_async_copy(x_ref, out_ref.at[dp, chip, core], own_sem)
    own.start()
    greet(sizes, here, ("dp", "chip", "core"))
    base = 0
    for axis, part, source in (
        ("dp", out_ref.at[dp, chip, core], x_ref),
        ("chip", out_ref.at[:, chip, core], None),
        ("core", out_ref.at[:, :, core], None),
    ):
        source = part if source is None else source
        copies = send_all(sizes, here, axis, lambda other: source, part, send_sem, recv_sem, base)
        if axis == "dp":
            own.wait()
        for copy in copies:
            copy.wait()
        base += sizes[axis] - 1


def dispatch_kernel(x_ref, out_ref, send_sem, recv_sem, own_sem):
    sizes, here = places()
    dp, e = here["dp"], here["expert"]
    own = pltpu.make_async_copy(x_ref.at[e], out_ref.at[dp, e], own_sem)
    own.start()
    greet(sizes, here, ("expert", "dp"))
    copies = send_all(
        sizes, here, "expert", lambda other: x_ref.at[other], out_ref.at[dp, e],
        send_sem, recv_sem, 0,
    )
    own.wait()
    for copy in copies:
        copy.wait()
    copies = send_all(
        sizes, here, "dp", lambda other: out_ref.at[dp], out_ref.at[dp],
        send_sem, recv_sem, sizes["expert"] - 1,
    )
    for copy in copies:
        copy.wait()


def exchange_kernel(axis, position, x_ref, out_ref, send_sem, recv_sem, own_sem):
    sizes, here = places()
    me = here[axis]

    def source(other):
        return x_ref.at[(slice(None),) * position + (other,)]

    own = pltpu.make_async_copy(source(me), out_ref.at[me], own_sem)
    own.start()
    greet(sizes, here, (axis,))
    copies = send_all(sizes, here, axis, source, out_ref.at[me], send_sem, recv_sem, 0)
    own.wait()
    for copy in copies:
        copy.wait()


def remote_call(kernel, x, out_shape, copies, identity, name):
    anywhere = pl.BlockSpec(memory_space=pl.ANY)
    return pl.pallas_call(
        kernel,
        out_shape=jax.ShapeDtypeStruct(out_shape, x.dtype),
        in_specs=[anywhere],
        out_specs=anywhere,
        scratch_shapes=[
            pltpu.SemaphoreType.DMA((copies,)),
            pltpu.SemaphoreType.DMA((copies,)),
            pltpu.SemaphoreType.DMA,
        ],
        compiler_params=pltpu.CompilerParams(collective_id=identity, has_side_effects=True),
        name=name,
    )(x)


def exchange(x, axis, position, identity, name):
    count = x.shape[position]
    rest = x.shape[:position] + x.shape[position + 1 :]
    return remote_call(
        functools.partial(exchange_kernel, axis, position), x, (count,) + rest, count - 1,
        identity, name,
    )


def gather_weights(packed):
    data, experts_axis = lax.axis_size("dp"), lax.axis_size("expert")
    chips = experts_axis // CORES
    shard, total = packed.shape
    full = remote_call(
        weights_kernel, packed, (data, chips, CORES, shard, total),
        data - 1 + chips - 1 + CORES - 1, 0, "gather_weights",
    )
    return full.reshape(data * experts_axis * shard, total)


def scatter_grads(grads):
    data, experts_axis = lax.axis_size("dp"), lax.axis_size("expert")
    chips = experts_axis // CORES
    rows, total = grads.shape
    x = grads.reshape(data, chips, CORES, rows // (data * experts_axis), total)
    x = jnp.sum(exchange(x, "core", 2, 1, "grads_core").astype(F32), axis=0).astype(BF16)
    x = jnp.sum(exchange(x, "chip", 1, 2, "grads_chip").astype(F32), axis=0).astype(BF16)
    return jnp.sum(exchange(x, "dp", 0, 3, "grads_data").astype(F32), axis=0)


def dispatch(send, experts, capacity):
    data, peers = lax.axis_size("dp"), lax.axis_size("expert")
    width = send.shape[1]
    local_count = experts // peers
    both = remote_call(
        dispatch_kernel, send.reshape(peers, local_count * capacity, width),
        (data, peers, local_count * capacity, width), data - 1 + peers - 1, 4, "dispatch_rows",
    )
    grouped = jnp.moveaxis(both.reshape(data * peers, local_count, capacity, width), 1, 0)
    return grouped.reshape(local_count, data * peers * capacity, width)


def collect(partial, experts, capacity):
    data, peers = lax.axis_size("dp"), lax.axis_size("expert")
    local_count, _, width = partial.shape
    grouped = jnp.moveaxis(partial.reshape(local_count, data * peers, capacity, width), 0, 1)
    grouped = grouped.reshape(data, peers, local_count * capacity, width)
    mine = jnp.sum(exchange(grouped, "dp", 0, 5, "return_data").astype(F32), axis=0).astype(BF16)
    back = exchange(mine, "expert", 0, 6, "return_rows")
    return back.reshape(experts * capacity, width)


def local(
    tokens, qkv_weight, out_weight, router_weight, norm_gains, bias_table,
    expert_in, expert_out, expert_ids, seq_lengths, bucket_ids, cotangent,
):
    rows, d = tokens.shape
    experts = router_weight.shape[1]
    shard = qkv_weight.shape[0]
    parts = d // shard
    capacity = max(2, 5 * rows // (4 * experts))
    table_cols = -(-BUCKETS * H // shard)
    used = experts + 2 + table_cols
    misc = -(-used // LANES) * LANES
    total = 4 * d + misc

    packed = jnp.concatenate(
        [qkv_weight, out_weight, router_weight, norm_gains,
         jnp.zeros((shard, misc - experts - 2), BF16)], axis=1,
    )
    weights = gather_weights(packed)
    gains = jnp.transpose(weights[:, 4 * d + experts : 4 * d + experts + 2]).astype(F32)
    half = rows // 2
    ring = jnp.concatenate(
        [bucket_ids[half - 1 :], jnp.full((1,), -1, jnp.int32), bucket_ids[: half - 1]]
    )
    hot = (ring[None, :] == jnp.arange(BUCKETS, dtype=jnp.int32)[:, None]).astype(F32)
    rel = lax.dot_general(bias_table, hot, (((0,), (0,)), ((), ())), precision=PRECISE)

    kept_shapes = (
        jax.ShapeDtypeStruct((rows, d), BF16),
        jax.ShapeDtypeStruct((rows, 3 * d), BF16),
        jax.ShapeDtypeStruct((H, rows, rows), F32),
        jax.ShapeDtypeStruct((rows, d), BF16),
        jax.ShapeDtypeStruct((rows, d), F32),
        jax.ShapeDtypeStruct((rows, experts), F32),
        jax.ShapeDtypeStruct((experts * capacity, 2 * d), BF16),
    )
    vm = pl.BlockSpec(memory_space=VMEM)
    *kept, send = pl.pallas_call(
        functools.partial(forward_kernel, d, experts, capacity),
        out_shape=kept_shapes,
        in_specs=[pl.BlockSpec(memory_space=pltpu.SMEM)] + [vm] * 6,
        out_specs=[vm] * 7,
        compiler_params=pltpu.CompilerParams(vmem_limit_bytes=BIG),
        name="attention_forward",
    )(seq_lengths, tokens, weights, gains, rel, expert_ids, cotangent)

    both = dispatch(send, experts, capacity)
    rows_in, grad_in = both[..., :d], both[..., d:]
    pre = jnp.einsum("aou,ahu->aoh", rows_in, expert_in, preferred_element_type=F32)
    act, act_back = jax.vjp(jax.nn.gelu, pre)
    hidden = act.astype(BF16)
    grad_hidden = jnp.einsum("aou,ahu->aoh", grad_in, expert_out, preferred_element_type=F32)
    grad_pre = act_back(grad_hidden)[0].astype(BF16)
    part_out = jnp.einsum("ziq,zqb->zib", hidden, expert_out, preferred_element_type=F32)
    part_grad = jnp.einsum("ziq,zqb->zib", grad_pre, expert_in, preferred_element_type=F32)
    partial = jnp.concatenate([part_out.astype(BF16), part_grad.astype(BF16)], axis=-1)
    ret = collect(partial, experts, capacity)
    grad_expert_in = jnp.einsum("ieq,ieo->iqo", grad_pre, rows_in, preferred_element_type=F32)
    grad_expert_out = jnp.einsum("ieq,ieo->iqo", hidden, grad_in, preferred_element_type=F32)

    mixed, grad_tokens, grads, grel = pl.pallas_call(
        functools.partial(backward_kernel, d, experts, capacity),
        out_shape=(
            jax.ShapeDtypeStruct((rows, d), BF16),
            jax.ShapeDtypeStruct((rows, d), F32),
            jax.ShapeDtypeStruct((d, total), BF16),
            jax.ShapeDtypeStruct((H, LANES), F32),
        ),
        in_specs=[vm] * 12,
        out_specs=[vm] * 4,
        scratch_shapes=[VMEM((rows, 3 * d), BF16)],
        compiler_params=pltpu.CompilerParams(vmem_limit_bytes=BIG),
        name="attention_backward",
    )(tokens, weights, gains, expert_ids, cotangent, *kept, ret)

    table = lax.dot_general(hot, grel, (((1,), (1,)), ((), ())), precision=PRECISE)
    tile = jnp.pad(table.reshape(-1), (0, shard * table_cols - BUCKETS * H))
    tile = jnp.tile(tile.reshape(shard, table_cols).astype(BF16), (parts, 1))
    grads = lax.dynamic_update_slice(grads, tile, (0, 4 * d + experts + 2))
    summed = scatter_grads(grads)
    at = 4 * d + experts
    table_sum = summed[:, at + 2 : at + 2 + table_cols].reshape(-1)[: BUCKETS * H]
    return (
        mixed,
        grad_tokens,
        summed[:, : 3 * d],
        summed[:, 3 * d : 4 * d],
        summed[:, 4 * d : at],
        summed[:, at : at + 2],
        table_sum.reshape(BUCKETS, H),
        grad_expert_in,
        grad_expert_out,
    )


def solution(mesh):
    both = P(("dp", "expert"), None)
    wide = P("expert", "dp", None)
    return jax.shard_map(
        local,
        mesh=mesh,
        in_specs=(both, both, both, both, both, P(), wide, wide, both, both, P(), both),
        out_specs=(both, both, both, both, both, both, P(), wide, wide),
        check_vma=False,
    )
```

```python
import functools

import jax
import jax.numpy as jnp
from jax import lax
from jax.experimental import pallas as pl
from jax.experimental.pallas import tpu as pltpu
from jax.sharding import PartitionSpec as P

H = 12
HD = 64
BUCKETS = 32
LANES = 128
EPSILON = 1e-06
NEGATIVE = -1e30
PRECISE = lax.Precision.HIGHEST
F32 = jnp.float32
BF16 = jnp.bfloat16
VMEM = pltpu.VMEM
BIG = 56 * 1024 * 1024


def mm(a, b, dims=((1,), (0,)), precision=None):
    return lax.dot_general(a, b, (dims, ((), ())), preferred_element_type=F32, precision=precision)


NT = ((1,), (1,))
TN = ((0,), (0,))


def rms_inverse(values):
    return lax.rsqrt(jnp.mean(values * values, axis=-1, keepdims=True) + EPSILON)


def placement(ids, experts, capacity):
    rows = ids.shape[0]
    picked = (ids == lax.broadcasted_iota(jnp.int32, (rows, experts), 1)).astype(F32)
    before = lax.broadcasted_iota(jnp.int32, (rows, rows), 1) < lax.broadcasted_iota(
        jnp.int32, (rows, rows), 0
    )
    earlier = mm(before.astype(BF16), picked.astype(BF16))
    slot = jnp.sum(earlier * picked, axis=-1, keepdims=True).astype(jnp.int32)
    flat = ids * capacity + slot
    place = (flat == lax.broadcasted_iota(jnp.int32, (rows, experts * capacity), 1)).astype(BF16)
    return picked, place


def forward_kernel(
    model_dim, experts, capacity,
    lens_ref, tok_ref, w_ref, gains_ref, rel_ref, ids_ref, cot_ref,
    normed_ref, qkv_ref, probs_ref, att_ref, res_ref, route_ref, send_ref,
):
    d = model_dim
    rows = tok_ref.shape[0]
    x = tok_ref[...].astype(F32)
    normed_ref[...] = (x * rms_inverse(x) * gains_ref[0:1, :]).astype(BF16)
    for c in range(0, 3 * d, 256):
        qkv_ref[:, c : c + 256] = mm(normed_ref[...], w_ref[:, c : c + 256]).astype(BF16)
    first = lens_ref[0, 0]
    second = first + lens_ref[0, 1]

    def segment(axis):
        pos = lax.broadcasted_iota(jnp.int32, (rows, rows), axis)
        return (pos >= first).astype(jnp.int32) + (pos >= second).astype(jnp.int32)

    same = segment(0) == segment(1)
    lane = lax.broadcasted_iota(jnp.int32, (rows, LANES), 1)
    for pair in range(H // 2):
        at = pair * LANES
        q = qkv_ref[:, at : at + LANES]
        k = qkv_ref[:, d + at : d + at + LANES]
        v = qkv_ref[:, 2 * d + at : 2 * d + at + LANES]
        outs = []
        for half in range(2):
            h = 2 * pair + half
            mine = (lane >= HD) if half else (lane < HD)
            bias = pltpu.roll(
                jnp.broadcast_to(rel_ref[h : h + 1, :], (rows, LANES)), 0, 1, stride=1, stride_axis=0
            )
            scores = mm(jnp.where(mine, q, jnp.zeros_like(q)), k, NT) * (HD ** (-0.5)) + bias
            scores = jnp.where(same, scores, NEGATIVE)
            e = jnp.exp(scores - jnp.max(scores, axis=-1, keepdims=True))
            p = e / jnp.sum(e, axis=-1, keepdims=True)
            probs_ref[h] = p
            outs.append(mm(p.astype(BF16), v))
        att_ref[:, at : at + LANES] = jnp.where(lane < HD, outs[0], outs[1]).astype(BF16)
    res = x + mm(att_ref[...], w_ref[:, 3 * d : 4 * d])
    res_ref[...] = res
    routed = (res * rms_inverse(res) * gains_ref[1:2, :]).astype(BF16)
    logits = mm(routed, w_ref[:, 4 * d :])[:, :experts]
    e = jnp.exp(logits - jnp.max(logits, axis=-1, keepdims=True))
    route = e / jnp.sum(e, axis=-1, keepdims=True)
    route_ref[...] = route
    picked, place = placement(ids_ref[...], experts, capacity)
    gate = jnp.sum(route * picked, axis=-1, keepdims=True)
    grad_comb = (gate * cot_ref[...].astype(F32)).astype(BF16)
    send_ref[:, :d] = mm(place, routed, TN).astype(BF16)
    send_ref[:, d:] = mm(place, grad_comb, TN).astype(BF16)


def backward_kernel(
    model_dim, experts, capacity,
    tok_ref, w_ref, gains_ref, ids_ref, cot_ref,
    normed_ref, qkv_ref, probs_ref, att_ref, res_ref, route_ref, ret_ref,
    mixed_ref, gtok_ref, grads_ref, grel_ref, grows_ref,
):
    d = model_dim
    rows = tok_ref.shape[0]
    x = tok_ref[...].astype(F32)
    g = cot_ref[...].astype(F32)
    res = res_ref[...]
    route = route_ref[...]
    picked, place = placement(ids_ref[...], experts, capacity)
    gate = jnp.sum(route * picked, axis=-1, keepdims=True)
    combined = mm(place, ret_ref[:, :d])
    mixed_ref[...] = (res + gate * combined).astype(BF16)
    grad_gate = jnp.sum(g * combined, axis=-1, keepdims=True)
    misc = w_ref.shape[1] - 4 * d
    glog = (grad_gate * gate * (picked - route)).astype(BF16)
    glog = jnp.concatenate([glog, jnp.zeros((rows, misc - experts), BF16)], axis=1)
    grouted = mm(place, ret_ref[:, d:]) + mm(glog, w_ref[:, 4 * d :], NT)
    inv2 = rms_inverse(res)
    scaled2 = res * inv2
    gain2 = gains_ref[1:2, :]
    routed = (scaled2 * gain2).astype(BF16)
    w = grouted * gain2
    gres = g + inv2 * (w - scaled2 * jnp.mean(w * scaled2, axis=-1, keepdims=True))
    col = lax.broadcasted_iota(jnp.int32, (rows, misc), 1)
    small = mm(routed, glog, TN) + mm(
        grouted * scaled2, (col == experts + 1).astype(F32), TN, PRECISE
    )
    branch = gres.astype(BF16)
    grads_ref[:, 3 * d : 4 * d] = mm(att_ref[...], branch, TN).astype(BF16)
    gatt = mm(branch, w_ref[:, 3 * d : 4 * d], NT).astype(BF16)
    lane = lax.broadcasted_iota(jnp.int32, (rows, LANES), 1)
    line = lax.broadcasted_iota(jnp.int32, (rows, LANES), 0)
    scale = HD ** (-0.5)
    for pair in range(H // 2):
        at = pair * LANES
        q = qkv_ref[:, at : at + LANES]
        k = qkv_ref[:, d + at : d + at + LANES]
        v = qkv_ref[:, 2 * d + at : 2 * d + at + LANES]
        ga = gatt[:, at : at + LANES]
        gq, gk, gv = [], [], []
        for half in range(2):
            h = 2 * pair + half
            mine = (lane >= HD) if half else (lane < HD)
            p = probs_ref[h]
            gp = mm(jnp.where(mine, ga, jnp.zeros_like(ga)), v, NT)
            gs = p * (gp - jnp.sum(p * gp, axis=-1, keepdims=True))
            low = gs.astype(BF16)
            gv.append(mm(p.astype(BF16), ga, TN))
            gq.append(mm(low, k) * scale)
            gk.append(mm(low, q, TN) * scale)
            step = 1
            while step < rows:
                turned = pltpu.roll(gs, LANES - step, 1)
                gs = jnp.where((line & step) != 0, turned, gs)
                step *= 2
            grel_ref[h : h + 1, :] = jnp.sum(gs, axis=0, keepdims=True)
        for base, two in ((0, gq), (d, gk), (2 * d, gv)):
            grows_ref[:, base + at : base + at + LANES] = jnp.where(
                lane < HD, two[0], two[1]
            ).astype(BF16)
    for c in range(0, 3 * d, 256):
        grads_ref[:, c : c + 256] = mm(normed_ref[...], grows_ref[:, c : c + 256], TN).astype(BF16)
    gnorm = mm(grows_ref[...], w_ref[:, : 3 * d], NT)
    inv1 = rms_inverse(x)
    scaled1 = x * inv1
    w = gnorm * gains_ref[0:1, :]
    gtok_ref[...] = gres + inv1 * (w - scaled1 * jnp.mean(w * scaled1, axis=-1, keepdims=True))
    small = small + mm(gnorm * scaled1, (col == experts).astype(F32), TN, PRECISE)
    grads_ref[:, 4 * d :] = small.astype(BF16)


CORES = 2
MESH = pl.DeviceIdType.MESH


def places():
    experts_axis = lax.axis_size("expert")
    sizes = {"dp": lax.axis_size("dp"), "chip": experts_axis // CORES, "core": CORES,
             "expert": experts_axis}
    e = lax.axis_index("expert")
    here = {"dp": lax.axis_index("dp"), "chip": e // CORES, "core": lax.rem(e, CORES), "expert": e}
    return sizes, here


def peer_of(here, axis, other):
    if axis == "dp":
        return (other, here["expert"])
    if axis == "chip":
        return (here["dp"], other * CORES + here["core"])
    if axis == "core":
        return (here["dp"], here["chip"] * CORES + other)
    return (here["dp"], other)


def greet(sizes, here, axes):
    barrier = pltpu.get_barrier_semaphore()
    count = 0
    for axis in axes:
        for k in range(1, sizes[axis]):
            other = lax.rem(here[axis] + k, sizes[axis])
            pl.semaphore_signal(
                barrier, inc=1, device_id=peer_of(here, axis, other), device_id_type=MESH
            )
            count += 1
    pl.semaphore_wait(barrier, count)


def send_all(sizes, here, axis, source, target, send_sem, recv_sem, base):
    copies = []
    for k in range(1, sizes[axis]):
        other = lax.rem(here[axis] + k, sizes[axis])
        copy = pltpu.make_async_remote_copy(
            src_ref=source(other), dst_ref=target,
            send_sem=send_sem.at[base + k - 1], recv_sem=recv_sem.at[base + k - 1],
            device_id=peer_of(here, axis, other), device_id_type=MESH,
        )
        copy.start()
        copies.append(copy)
    return copies


def weights_kernel(x_ref, out_ref, send_sem, recv_sem, own_sem):
    sizes, here = places()
    dp, chip, core = here["dp"], here["chip"], here["core"]
    own = pltpu.make_async_copy(x_ref, out_ref.at[dp, chip, core], own_sem)
    own.start()
    greet(sizes, here, ("dp", "chip", "core"))
    base = 0
    for axis, part, source in (
        ("dp", out_ref.at[dp, chip, core], x_ref),
        ("chip", out_ref.at[:, chip, core], None),
        ("core", out_ref.at[:, :, core], None),
    ):
        source = part if source is None else source
        copies = send_all(sizes, here, axis, lambda other: source, part, send_sem, recv_sem, base)
        if axis == "dp":
            own.wait()
        for copy in copies:
            copy.wait()
        base += sizes[axis] - 1


def swap_kernel(axis, position, x_ref, out_ref, send_sem, recv_sem):
    sizes, here = places()
    greet(sizes, here, (axis,))
    copies = []
    for k in range(1, sizes[axis]):
        other = lax.rem(here[axis] + k, sizes[axis])
        copy = pltpu.make_async_remote_copy(
            src_ref=x_ref.at[(slice(None),) * position + (other,)], dst_ref=out_ref.at[k - 1],
            send_sem=send_sem.at[k - 1], recv_sem=recv_sem.at[k - 1],
            device_id=peer_of(here, axis, other), device_id_type=MESH,
        )
        copy.start()
        copies.append(copy)
    for copy in copies:
        copy.wait()


def rows_kernel(x_ref, out_ref, send_sem, recv_sem, own_sem):
    sizes, here = places()
    e = here["expert"]
    own = pltpu.make_async_copy(x_ref.at[e], out_ref.at[e], own_sem)
    own.start()
    greet(sizes, here, ("expert",))
    copies = send_all(
        sizes, here, "expert", lambda other: x_ref.at[other], out_ref.at[e], send_sem, recv_sem, 0
    )
    own.wait()
    for copy in copies:
        copy.wait()


def remote_call(kernel, x, out_shape, copies, identity, name, keeps_own=True):
    anywhere = pl.BlockSpec(memory_space=pl.ANY)
    return pl.pallas_call(
        kernel,
        out_shape=jax.ShapeDtypeStruct(out_shape, x.dtype),
        in_specs=[anywhere],
        out_specs=anywhere,
        scratch_shapes=[
            pltpu.SemaphoreType.DMA((copies,)),
            pltpu.SemaphoreType.DMA((copies,)),
        ] + ([pltpu.SemaphoreType.DMA] if keeps_own else []),
        compiler_params=pltpu.CompilerParams(collective_id=identity, has_side_effects=True),
        name=name,
    )(x)


def swap_sum(x, axis, position, identity, name):
    _, here = places()
    count = x.shape[position]
    rest = x.shape[:position] + x.shape[position + 1 :]
    got = remote_call(
        functools.partial(swap_kernel, axis, position), x, (count - 1,) + rest, count - 1,
        identity, name, keeps_own=False,
    )
    total = lax.dynamic_index_in_dim(x, here[axis], position, keepdims=False).astype(F32)
    for k in range(count - 1):
        total = total + got[k].astype(F32)
    return total


def swap_rows(x, identity, name):
    return remote_call(rows_kernel, x, x.shape, x.shape[0] - 1, identity, name)


def gather_weights(packed):
    data, experts_axis = lax.axis_size("dp"), lax.axis_size("expert")
    chips = experts_axis // CORES
    shard, total = packed.shape
    full = remote_call(
        weights_kernel, packed, (data, chips, CORES, shard, total),
        data - 1 + chips - 1 + CORES - 1, 0, "gather_weights",
    )
    return full.reshape(data * experts_axis * shard, total)


def scatter_grads(grads):
    data, experts_axis = lax.axis_size("dp"), lax.axis_size("expert")
    chips = experts_axis // CORES
    rows, total = grads.shape
    x = grads.reshape(data, chips, CORES, rows // (data * experts_axis), total)
    x = swap_sum(x, "core", 2, 1, "grads_core").astype(BF16)
    x = swap_sum(x, "chip", 1, 2, "grads_chip").astype(BF16)
    return swap_sum(x, "dp", 0, 3, "grads_data")


def dispatch(send, experts, capacity):
    peers = lax.axis_size("expert")
    width = send.shape[1]
    local_count = experts // peers
    arrived = swap_rows(
        send.reshape(peers, local_count * capacity, width), 4, "dispatch_rows"
    )
    grouped = jnp.moveaxis(arrived.reshape(peers, local_count, capacity, width), 1, 0)
    grouped = grouped.reshape(local_count, peers * capacity, width)
    return lax.all_gather(grouped, "dp", axis=1, tiled=True)


def collect(partial, experts, capacity):
    peers = lax.axis_size("expert")
    local_count, _, width = partial.shape
    mine = lax.psum_scatter(partial, "dp", scatter_dimension=1, tiled=True)
    grouped = jnp.moveaxis(mine.reshape(local_count, peers, capacity, width), 0, 1)
    back = swap_rows(grouped.reshape(peers, local_count * capacity, width), 5, "return_rows")
    return back.reshape(experts * capacity, width)


def local(
    tokens, qkv_weight, out_weight, router_weight, norm_gains, bias_table,
    expert_in, expert_out, expert_ids, seq_lengths, bucket_ids, cotangent,
):
    rows, d = tokens.shape
    experts = router_weight.shape[1]
    shard = qkv_weight.shape[0]
    parts = d // shard
    capacity = max(2, 5 * rows // (4 * experts))
    table_cols = -(-BUCKETS * H // shard)
    used = experts + 2 + table_cols
    misc = -(-used // LANES) * LANES
    total = 4 * d + misc

    packed = jnp.concatenate(
        [qkv_weight, out_weight, router_weight, norm_gains,
         jnp.zeros((shard, misc - experts - 2), BF16)], axis=1,
    )
    weights = gather_weights(packed)
    gains = jnp.transpose(weights[:, 4 * d + experts : 4 * d + experts + 2]).astype(F32)
    half = rows // 2
    ring = jnp.concatenate(
        [bucket_ids[half - 1 :], jnp.full((1,), -1, jnp.int32), bucket_ids[: half - 1]]
    )
    hot = (ring[None, :] == jnp.arange(BUCKETS, dtype=jnp.int32)[:, None]).astype(F32)
    rel = lax.dot_general(bias_table, hot, (((0,), (0,)), ((), ())), precision=PRECISE)

    kept_shapes = (
        jax.ShapeDtypeStruct((rows, d), BF16),
        jax.ShapeDtypeStruct((rows, 3 * d), BF16),
        jax.ShapeDtypeStruct((H, rows, rows), F32),
        jax.ShapeDtypeStruct((rows, d), BF16),
        jax.ShapeDtypeStruct((rows, d), F32),
        jax.ShapeDtypeStruct((rows, experts), F32),
        jax.ShapeDtypeStruct((experts * capacity, 2 * d), BF16),
    )
    vm = pl.BlockSpec(memory_space=VMEM)
    *kept, send = pl.pallas_call(
        functools.partial(forward_kernel, d, experts, capacity),
        out_shape=kept_shapes,
        in_specs=[pl.BlockSpec(memory_space=pltpu.SMEM)] + [vm] * 6,
        out_specs=[vm] * 7,
        compiler_params=pltpu.CompilerParams(vmem_limit_bytes=BIG),
        name="attention_forward",
    )(seq_lengths, tokens, weights, gains, rel, expert_ids, cotangent)

    both = dispatch(send, experts, capacity)
    rows_in, grad_in = both[..., :d], both[..., d:]
    pre = jnp.einsum("aou,ahu->aoh", rows_in, expert_in, preferred_element_type=F32)
    act, act_back = jax.vjp(jax.nn.gelu, pre)
    hidden = act.astype(BF16)
    grad_hidden = jnp.einsum("aou,ahu->aoh", grad_in, expert_out, preferred_element_type=F32)
    grad_pre = act_back(grad_hidden)[0].astype(BF16)
    part_out = jnp.einsum("ziq,zqb->zib", hidden, expert_out, preferred_element_type=F32)
    part_grad = jnp.einsum("ziq,zqb->zib", grad_pre, expert_in, preferred_element_type=F32)
    partial = jnp.concatenate([part_out.astype(BF16), part_grad.astype(BF16)], axis=-1)
    ret = collect(partial, experts, capacity)
    grad_expert_in = jnp.einsum("ieq,ieo->iqo", grad_pre, rows_in, preferred_element_type=F32)
    grad_expert_out = jnp.einsum("ieq,ieo->iqo", hidden, grad_in, preferred_element_type=F32)

    mixed, grad_tokens, grads, grel = pl.pallas_call(
        functools.partial(backward_kernel, d, experts, capacity),
        out_shape=(
            jax.ShapeDtypeStruct((rows, d), BF16),
            jax.ShapeDtypeStruct((rows, d), F32),
            jax.ShapeDtypeStruct((d, total), BF16),
            jax.ShapeDtypeStruct((H, LANES), F32),
        ),
        in_specs=[vm] * 12,
        out_specs=[vm] * 4,
        scratch_shapes=[VMEM((rows, 3 * d), BF16)],
        compiler_params=pltpu.CompilerParams(vmem_limit_bytes=BIG),
        name="attention_backward",
    )(tokens, weights, gains, expert_ids, cotangent, *kept, ret)

    table = lax.dot_general(hot, grel, (((1,), (1,)), ((), ())), precision=PRECISE)
    tile = jnp.pad(table.reshape(-1), (0, shard * table_cols - BUCKETS * H))
    tile = jnp.tile(tile.reshape(shard, table_cols).astype(BF16), (parts, 1))
    grads = lax.dynamic_update_slice(grads, tile, (0, 4 * d + experts + 2))
    summed = scatter_grads(grads)
    at = 4 * d + experts
    table_sum = summed[:, at + 2 : at + 2 + table_cols].reshape(-1)[: BUCKETS * H]
    return (
        mixed,
        grad_tokens,
        summed[:, : 3 * d],
        summed[:, 3 * d : 4 * d],
        summed[:, 4 * d : at],
        summed[:, at : at + 2],
        table_sum.reshape(BUCKETS, H),
        grad_expert_in,
        grad_expert_out,
    )


def solution(mesh):
    both = P(("dp", "expert"), None)
    wide = P("expert", "dp", None)
    return jax.shard_map(
        local,
        mesh=mesh,
        in_specs=(both, both, both, both, both, P(), wide, wide, both, both, P(), both),
        out_specs=(both, both, both, both, both, both, P(), wide, wide),
        check_vma=False,
    )
```
